256 devices in a mesh: blk: 64 (over z_lo, x, y, core), grp: 4 (over z_hi).
Axes of the slice: x: 4, y: 4, z: 8 (z_hi: 4, z_lo: 2; z = z_hi * 2 + z_lo), core: 2. Of those that a mesh axis runs over, the one named last changes fastest.
Arguments:
- queries: bfloat16 [65536, 4096], P(('blk', 'grp')), may hold values from -1 to 1
- documents: bfloat16 [65536, 4096], P(('blk', 'grp')), may hold values from -1 to 1
- positives: int32 [256, 256], P(('blk', 'grp')), may hold values from 0 to 255, as said below
Outputs:
- query_grad: float32 [65536, 4096], P(('blk', 'grp'))
- doc_grad: float32 [65536, 4096], P(('blk', 'grp'))
- loss: float32 [], replicated
The draws below stay inside these ranges and needn't reach their ends.
Inputs may be any that keep to these rules, and one draw needn't show every extreme that they name: `positives`: each block of 256 rows names each of 0 to 255 exactly once.
All inputs are finite; a program needn't handle non-finite values.
Results may differ from the reference program's by a relative error of at most 0.0036.
Values may be sent and summed in bfloat16 or wider, within the bound.
No kernel may reach another device: no remote copies, remote signals or barrier semaphores. Data moves between devices by JAX's collectives and lax.ppermute only.
A program may use at most 128 MiB of HBM per device.

```python
import jax
import jax.numpy as jnp
from jax import lax

D = 4096
ROWS = 256
TOTAL = 65536
N_BLK = 64
N_GRP = 4


def common_draw(key):
    key_noise = jax.random.fold_in(key, 11)
    key_docs = jax.random.fold_in(key, 12)
    key_perm = jax.random.fold_in(key, 13)
    blocks = N_BLK * N_GRP
    perm_keys = jax.random.split(key_perm, blocks)
    positives = jax.vmap(lambda k: jax.random.permutation(k, ROWS))(perm_keys).astype(jnp.int32)
    docs = jax.random.normal(key_docs, (TOTAL, D), jnp.float32) * D ** (-0.5)
    noise = jax.random.normal(key_noise, (TOTAL, D), jnp.float32) * D ** (-0.5)
    span = 0.12
    rows = jnp.arange(TOTAL, dtype=jnp.int32)
    block = rows // ROWS
    shard = (block // N_GRP).astype(jnp.float32)
    align = span * shard / (N_BLK - 1)
    target = block * ROWS + positives.reshape(-1)
    paired = docs[target]
    raw_q = jnp.sqrt(1.0 - align * align)[:, None] * noise + align[:, None] * paired
    return (raw_q, docs, positives)


def draw_queries(key, part):
    return common_draw(key)[0].astype(jnp.bfloat16)


def draw_documents(key, part):
    return common_draw(key)[1].astype(jnp.bfloat16)


def draw_positives(key, part):
    return common_draw(key)[2]


def setup_inputs(seed: int = 0) -> dict:
    keys = jax.random.split(jax.random.key(seed), 4)
    queries = draw_queries(jax.random.fold_in(keys[3], 71), 0)
    documents = draw_documents(jax.random.fold_in(keys[3], 71), 0)
    positives = draw_positives(jax.random.fold_in(keys[3], 71), 0)
    return {"queries": queries, "documents": documents, "positives": positives}


SCALE = 50.0
EPSILON = 1e-06

def normalize(raw):
    wide = raw.astype(jnp.float32)
    ratio = lax.rsqrt(lax.optimization_barrier(jnp.sum(wide * wide, axis=-1, keepdims=True)) + EPSILON)
    return ((wide * ratio).astype(jnp.bfloat16), ratio)

def pull_back(grad, wide, ratio):
    inner = lax.optimization_barrier(jnp.sum(wide * grad, axis=-1, keepdims=True))
    return ratio * grad - ratio * ratio * ratio * inner * wide

def reference(queries, documents, positives):
    far = N_BLK // 4
    offsets = [0, 1, -1, far, -far]
    norm_q, ratio_q = normalize(queries)
    norm_d, ratio_d = normalize(documents)
    eq4 = norm_q.reshape(N_BLK, N_GRP, ROWS, D)
    ed4 = norm_d.reshape(N_BLK, N_GRP, ROWS, D)
    rq4 = ratio_q.reshape(N_BLK, N_GRP, ROWS, 1)
    rd4 = ratio_d.reshape(N_BLK, N_GRP, ROWS, 1)
    raw_q = queries.reshape(N_BLK, N_GRP, ROWS, D)
    raw_d = documents.reshape(N_BLK, N_GRP, ROWS, D)
    pos4 = positives.reshape(N_BLK, N_GRP, ROWS)
    columns = jnp.arange(ROWS, dtype=jnp.int32)

    def hot_of(index):
        return (columns[None, None, :] == pos4[index][:, :, None]).astype(jnp.float32)

    def forward(index):
        cand = jnp.stack([ed4[jnp.mod(index - off, N_BLK).astype(jnp.int32)] for off in offsets]).astype(jnp.float32)
        left = eq4[index].astype(jnp.float32)
        scores = SCALE * jnp.einsum('gid,cgjd->cgij', left, cand)
        lse = jnp.log(lax.optimization_barrier(jnp.sum(jnp.exp(scores), axis=(0, 3))))
        hot = hot_of(index)
        spos = lax.optimization_barrier(jnp.sum(scores[0] * hot, axis=-1))
        part = jnp.sum(lse - spos)
        probs = jnp.exp(scores - lse[None, :, :, None])
        probs = jnp.concatenate([(probs[0] - hot)[None], probs[1:]], axis=0)
        weights = probs.astype(jnp.bfloat16).astype(jnp.float32)
        direction = SCALE * jnp.einsum('cgij,cgjd->gid', weights, cand)
        grad = pull_back(direction, raw_q[index].astype(jnp.float32), rq4[index])
        return (grad, lse, part)
    grads_q, lses, parts = lax.map(forward, jnp.arange(N_BLK, dtype=jnp.int32))

    def backward(index):
        right = ed4[index].astype(jnp.float32)
        total = jnp.zeros((N_GRP, ROWS, D), jnp.float32)
        for off in offsets:
            source = jnp.mod(index + off, N_BLK).astype(jnp.int32)
            left = eq4[source].astype(jnp.float32)
            scores = SCALE * jnp.einsum('gid,gjd->gij', left, right)
            probs = jnp.exp(scores - lses[source][:, :, None])
            if off == 0:
                probs = probs - hot_of(index)
            weights = probs.astype(jnp.bfloat16).astype(jnp.float32)
            total = total + SCALE * jnp.einsum('gij,gid->gjd', weights, left)
        return pull_back(total, raw_d[index].astype(jnp.float32), rd4[index])
    grads_d = lax.map(backward, jnp.arange(N_BLK, dtype=jnp.int32))
    loss = jnp.sum(parts) / TOTAL
    return (grads_q.reshape(TOTAL, D), grads_d.reshape(TOTAL, D), loss)
```

```python
import itertools

import jax
import jax.numpy as jnp
from jax import lax
from jax.experimental import pallas as pl
from jax.experimental.pallas import tpu as pltpu
from jax.sharding import Mesh
from jax.sharding import PartitionSpec as P

BLK = ("blk_0", "blk_1", "blk_2", "blk_3")
GRP = "grp"
BLK_GRP = BLK + (GRP,)
NZ, NX, NY, NC = 2, 4, 4, 2

SCALE = 50.0
EPSILON = 1e-06
DOC_CHUNKS = (128, 128)
QUERY_CHUNKS = (128, 128)
STRIPE = 1024
STEP = 64
MIB = 1024 * 1024


def index(z, x, y, c):
    return ((z % NZ * NX + x % NX) * NY + y % NY) * NC + c % NC


def table(target):
    pairs = []
    for at in itertools.product(range(NZ), range(NX), range(NY), range(NC)):
        to = target(*at)
        if to is not None:
            pairs.append((index(*at), index(*to)))
    return pairs


def is_edge(y, c):
    return (y == NY - 1 and c == 1) or (y == 0 and c == 0)


def off_chip(z, x, y, c):
    step = 1 if c == 1 else -1
    me = index(z, x, y, c)
    other = (me + step) % (NZ * NX * NY * NC)
    return (other // (NX * NY * NC), other // (NY * NC) % NX, other // NC % NY, other % NC)


def to_holder(z, x, y, c):
    if not is_edge(y, c):
        return None
    if c == 1:
        return (z + (x == NX - 1), x, 0, 0)
    return (z + (x == 0), x, NY - 1, 1)


def from_holder(z, x, y, c):
    if not is_edge(y, c):
        return off_chip(z, x, y, c)
    return (z, x + 1, y, c) if c == 0 else (z, x - 1, y, c)


ON_CHIP = table(lambda z, x, y, c: (z, x, y, 1 - c))
OFF_CHIP = table(off_chip)
TO_HOLDER = table(to_holder)
FROM_HOLDER = table(from_holder)
ACROSS_X = table(lambda z, x, y, c: (z, x + 2, y, c))
ACROSS_Z = table(lambda z, x, y, c: (z + 1, x, y, c))
ACROSS_XZ = table(lambda z, x, y, c: (z + 1, x + 2, y, c))


def permute(value, pairs):
    return lax.ppermute(value, BLK, pairs)


def after(value, *others):
    others = [o for o in others if o is not None]
    if not others:
        return value
    return lax.optimization_barrier((value, *others))[0]


ANY = pl.BlockSpec(memory_space=pl.ANY)
VMEM = pl.BlockSpec(memory_space=pltpu.VMEM)


def call(kernel, inputs, outputs, scratch, *, any_in, any_out):
    return pl.pallas_call(
        kernel,
        in_specs=[ANY if a else VMEM for a in any_in],
        out_specs=[ANY if a else VMEM for a in any_out],
        out_shape=outputs,
        scratch_shapes=scratch,
        cost_estimate=pl.CostEstimate(flops=1024, bytes_accessed=1024, transcendentals=0),
        compiler_params=pltpu.CompilerParams(vmem_limit_bytes=60 * MIB),
    )(*inputs)


def shape(rows, columns, kind):
    return jax.ShapeDtypeStruct((rows, columns), kind)


def start(source, target, sem):
    copy = pltpu.make_async_copy(source, target, sem)
    copy.start()
    return copy


def normalize(raw, chunks):
    rows, width = raw.shape
    spans = [(0, rows)]
    for sizes in chunks:
        spans += [(sum(sizes[:k]), size) for k, size in enumerate(sizes)]
    n, steps = len(spans), rows // STEP

    def kernel(raw, *refs):
        outs, ratio = refs[:n], refs[n]
        before, result, sems, out_sems = refs[n + 1 :]
        loads = [
            start(raw.at[pl.ds(k * STEP, STEP)], before.at[pl.ds(k * STEP, STEP)], sems.at[k])
            for k in range(steps)
        ]
        stores = []
        for k in range(steps):
            own = pl.ds(k * STEP, STEP)
            loads[k].wait()
            wide = before[own].astype(jnp.float32)
            scale = lax.rsqrt(jnp.sum(wide * wide, axis=-1, keepdims=True) + EPSILON)
            ratio[own] = scale
            result[own] = (wide * scale).astype(jnp.bfloat16)
            for j, (at, size) in enumerate(spans):
                if k * STEP < at + size <= (k + 1) * STEP:
                    stores.append(start(result.at[pl.ds(at, size)], outs[j], out_sems.at[j]))
        for copy in stores:
            copy.wait()

    kind = jnp.bfloat16
    return call(
        kernel,
        [raw],
        [shape(size, width, kind) for _, size in spans] + [shape(rows, 1, jnp.float32)],
        [
            pltpu.VMEM((rows, width), kind),
            pltpu.VMEM((rows, width), kind),
            pltpu.SemaphoreType.DMA((steps,)),
            pltpu.SemaphoreType.DMA((n,)),
        ],
        any_in=[True],
        any_out=[True] * n + [False],
    )


def places(blocks):
    at, found = 0, []
    for block in blocks:
        found.append((at, block.shape[0]))
        at += block.shape[0]
    return found, at


def diagonal(size):
    return lax.broadcasted_iota(jnp.int32, (size, size), 0) == lax.broadcasted_iota(
        jnp.int32, (size, size), 1
    )


def column_of(row):
    return jnp.sum(jnp.where(diagonal(row.shape[1]), row, 0), axis=1, keepdims=True)


def row_of(column):
    return jnp.sum(jnp.where(diagonal(column.shape[0]), column, 0), axis=0, keepdims=True)


def scores_of(own, block):
    return SCALE * lax.dot_general(
        own, block, (((1,), (1,)), ((), ())), preferred_element_type=jnp.float32
    )


def groups_of(found, rows):
    runs = []
    for k, (at, size) in enumerate(found):
        if runs and at + size - runs[-1][1] <= rows:
            runs[-1] = (runs[-1][0] + [k], runs[-1][1], at + size - runs[-1][1])
        else:
            runs.append(([k], at, size))
    return runs


def query_side(norm, positive, blocks):
    rows, width = norm.shape
    found, depth = places(blocks)
    n = len(blocks)

    def kernel(norm, positive, *refs):
        blocks, (lse_out, part_out, weights_out, inner_out) = refs[:n], refs[n : n + 4]
        own, buffer, scores, sems = refs[n + 4 :]
        first = start(norm, own, sems.at[n])
        loads = [
            start(blocks[k], buffer.at[pl.ds(at, size)], sems.at[k])
            for k, (at, size) in enumerate(found)
        ]
        first.wait()
        total = jnp.zeros((rows, 1), jnp.float32)
        for members, at, size in groups_of(found, rows):
            for k in members:
                loads[k].wait()
            here = scores_of(own[...], buffer[at : at + size])
            scores[:, at : at + size] = here
            total += jnp.sum(jnp.exp(here), axis=-1, keepdims=True)
        lse = jnp.log(total)
        lse_out[...] = row_of(lse)
        target = column_of(positive[...])
        spos = jnp.zeros((rows, 1), jnp.float32)
        inner = jnp.zeros((rows, 1), jnp.float32)
        for at in range(0, depth, rows):
            here = scores[:, at : at + rows]
            weights = jnp.exp(here - lse)
            if at < 2 * rows:
                hot = lax.broadcasted_iota(jnp.int32, (rows, rows), 1) + at == target
                hot = hot.astype(jnp.float32)
                spos += jnp.sum(here * hot, axis=-1, keepdims=True)
                weights = weights - hot
            weights = weights.astype(jnp.bfloat16)
            weights_out[:, at : at + rows] = weights
            inner += jnp.sum(weights.astype(jnp.float32) * here, axis=-1, keepdims=True)
        inner_out[...] = inner
        part = jnp.sum(lse - spos, axis=0, keepdims=True)
        part_out[...] = jnp.broadcast_to(part, part_out.shape)

    return call(
        kernel,
        [norm, positive, *blocks],
        [
            shape(1, rows, jnp.float32),
            shape(8, 128, jnp.float32),
            shape(rows, depth, jnp.bfloat16),
            shape(rows, 1, jnp.float32),
        ],
        [
            pltpu.VMEM((rows, width), jnp.bfloat16),
            pltpu.VMEM((depth, width), jnp.bfloat16),
            pltpu.VMEM((rows, depth), jnp.float32),
            pltpu.SemaphoreType.DMA((n + 1,)),
        ],
        any_in=[True, False] + [True] * n,
        any_out=[False] * 4,
    )


def query_gradient(weights, inner, ratio, raw, blocks):
    rows, width = raw.shape
    found, depth = places(blocks)
    n, stripes = len(blocks), width // STRIPE

    def kernel(weights, inner, ratio, raw, *refs):
        blocks, out, done = refs[:n], refs[n], refs[n + 1]
        buffer, wide, result, sems, out_sems = refs[n + 2 :]
        done[...] = jnp.zeros_like(done)
        loads = []
        for s in range(stripes):
            at_s = pl.ds(s * STRIPE, STRIPE)
            loads.append(
                [
                    start(blocks[k].at[:, at_s], buffer.at[pl.ds(at, size), at_s], sems.at[s, k])
                    for k, (at, size) in enumerate(found)
                ]
                + [start(raw.at[:, at_s], wide.at[:, at_s], sems.at[s, n])]
            )
        gain = SCALE * ratio[...]
        coef = ratio[...] * ratio[...] * inner[...]
        stores = []
        for s in range(stripes):
            here = slice(s * STRIPE, (s + 1) * STRIPE)
            for copy in loads[s]:
                copy.wait()
            direction = jnp.dot(weights[...], buffer[:, here], preferred_element_type=jnp.float32)
            result[:, here] = gain * direction - coef * wide[:, here].astype(jnp.float32)
            at_s = pl.ds(s * STRIPE, STRIPE)
            stores.append(start(result.at[:, at_s], out.at[:, at_s], out_sems.at[s]))
        for copy in stores:
            copy.wait()

    return call(
        kernel,
        [weights, inner, ratio, raw, *blocks],
        [shape(rows, width, jnp.float32), shape(8, 128, jnp.float32)],
        [
            pltpu.VMEM((depth, width), jnp.bfloat16),
            pltpu.VMEM((rows, width), jnp.bfloat16),
            pltpu.VMEM((rows, width), jnp.float32),
            pltpu.SemaphoreType.DMA((stripes, n + 1)),
            pltpu.SemaphoreType.DMA((stripes,)),
        ],
        any_in=[False] * 3 + [True] * (n + 1),
        any_out=[True, False],
    )


def document_side(norm, positive, lses, blocks, last=None):
    rows, width = norm.shape
    found, depth = places(blocks)
    n, stripes = len(blocks), width // STRIPE
    given = [] if positive is None else [positive]
    small = given + [lses] + ([] if last is None else [last[0], last[3]])
    large = [norm, *blocks] + ([] if last is None else [last[1], last[2]])
    m = len(small)

    def kernel(*refs):
        smalls, (norm, *blocks) = refs[:m], refs[m : m + 1 + n]
        rest = refs[m + 1 + n :]
        lses = smalls[len(given)]
        if last is not None:
            ratio, before_inner = smalls[-2:]
            raw, before = rest[:2]
            rest = rest[2:]
        out, rest = rest[0], rest[1:]
        if last is None:
            inner_out, rest = rest[0], rest[1:]
        own, buffer, result, wide, sems, more_sems, out_sems = rest
        first = start(norm, own, sems.at[n])
        loads = [
            start(blocks[k], buffer.at[pl.ds(at, size)], sems.at[k])
            for k, (at, size) in enumerate(found)
        ]
        more = []
        if last is not None:
            for s in range(stripes):
                at_s = pl.ds(s * STRIPE, STRIPE)
                more.append(
                    [
                        start(raw.at[:, at_s], wide.at[:, at_s], more_sems.at[s, 0]),
                        start(before.at[:, at_s], result.at[:, at_s], more_sems.at[s, 1]),
                    ]
                )
        first.wait()
        inner = jnp.zeros((rows, 1), jnp.float32) if last is None else before_inner[...]
        weights = []
        for members, at, size in groups_of(found, rows):
            for k in members:
                loads[k].wait()
            here = scores_of(own[...], buffer[at : at + size])
            weight = jnp.exp(here - lses[:, at : at + size])
            if at < 2 * rows and given:
                hot = lax.broadcasted_iota(jnp.int32, (rows, size), 0)
                hot = hot == smalls[0][:, at : at + size]
                weight = weight - hot.astype(jnp.float32)
            weight = weight.astype(jnp.bfloat16)
            inner += jnp.sum(weight.astype(jnp.float32) * here, axis=-1, keepdims=True)
            weights.append((weight, at, size))
        if last is None:
            inner_out[...] = inner
        else:
            gain = SCALE * ratio[...]
            coef = ratio[...] * ratio[...] * inner
        stores = []
        for s in range(stripes):
            here = slice(s * STRIPE, (s + 1) * STRIPE)
            direction = None
            for weight, at, size in weights:
                term = jnp.dot(
                    weight, buffer[at : at + size, here], preferred_element_type=jnp.float32
                )
                direction = term if direction is None else direction + term
            if last is not None:
                for copy in more[s]:
                    copy.wait()
                direction = gain * (direction + result[:, here])
                direction = direction - coef * wide[:, here].astype(jnp.float32)
            result[:, here] = direction
            at_s = pl.ds(s * STRIPE, STRIPE)
            stores.append(start(result.at[:, at_s], out.at[:, at_s], out_sems.at[s]))
        for copy in stores:
            copy.wait()

    outputs = [shape(rows, width, jnp.float32)]
    if last is None:
        outputs.append(shape(rows, 1, jnp.float32))
    return call(
        kernel,
        small + large,
        outputs,
        [
            pltpu.VMEM((rows, width), jnp.bfloat16),
            pltpu.VMEM((depth, width), jnp.bfloat16),
            pltpu.VMEM((rows, width), jnp.float32),
            pltpu.VMEM((rows, width), jnp.bfloat16),
            pltpu.SemaphoreType.DMA((n + 1,)),
            pltpu.SemaphoreType.DMA((stripes, 2)),
            pltpu.SemaphoreType.DMA((stripes,)),
        ],
        any_in=[False] * m + [True] * len(large),
        any_out=[True] + [False] * (last is None),
    )


def total_over(value, axes):
    count = 1
    for axis in axes:
        count *= lax.axis_size(axis)
    parts = [
        lax.ppermute(value, axes, [(s, (s + step) % count) for s in range(count)])
        for step in range(1, count)
    ]
    for part in parts:
        value = value + part
    return value


def on_device(queries, documents, positives):
    rows = queries.shape[0]
    y = lax.axis_index("blk_2")
    c = lax.axis_index("blk_3")
    edge = ((y == NY - 1) & (c == 1)) | ((y == 0) & (c == 0))
    n, tail = len(DOC_CHUNKS), QUERY_CHUNKS[-1]
    halves = (rows // 2, rows // 2)

    norm_d, *pieces_d, ratio_d = normalize(documents, [DOC_CHUNKS, halves])
    norm_q, *pieces_q, ratio_q = normalize(queries, [QUERY_CHUNKS])
    halves_d, pieces_d = pieces_d[-2:], pieces_d[:-2]

    pair_d = lax.all_gather(norm_d, "blk_3", tiled=True)
    pair_q = lax.all_gather(norm_q, "blk_3", tiled=True)

    far, farther = [], []
    for k, part in enumerate(pieces_d + pieces_q):
        gates = [] if k < 2 else far[:2] + farther[:1]
        far.append(permute(after(part, *gates), ACROSS_X))
        farther.append(permute(far[k], ACROSS_Z))

    held_d = permute(halves_d[1], TO_HOLDER)
    near_d = [
        permute(after(halves_d[0], far[1]), OFF_CHIP),
        permute(after(jnp.where(edge, held_d, halves_d[1]), far[1]), FROM_HOLDER),
    ]
    held_q = permute(after(norm_q, held_d), TO_HOLDER)
    near_q = permute(after(jnp.where(edge, held_q, norm_q), far[-1]), FROM_HOLDER)

    docs = [pair_d, *near_d] + far[:n] + farther[:n]
    target = jnp.where(c == 0, positives, positives + rows)
    lse, part, weights, inner = query_side(norm_q, target, docs)

    message = after(lse, farther[n])
    other = permute(message, ON_CHIP)
    near_lse = permute(message, OFF_CHIP)
    far_lse = permute(message, ACROSS_X)
    farther_lse = permute(message, ACROSS_XZ)
    none = jnp.full_like(positives, -1)
    first = jnp.where(c == 0, lse, other)
    second = jnp.where(c == 0, other, lse)
    marks = jnp.where(c == 0, jnp.concatenate([positives, none], 1), jnp.concatenate([none, positives], 1))

    query_grad, done = query_gradient(weights, inner, ratio_q, queries, docs)
    early = jnp.concatenate([first, second, far_lse, farther_lse[:, :-tail]], axis=1)
    early = after(early, query_grad)
    direction, inner = document_side(norm_d, marks, early, [pair_q] + far[n:] + farther[n:-1])
    late = jnp.concatenate([near_lse, farther_lse[:, -tail:]], axis=1)
    doc_grad = document_side(
        norm_d, None, late, [near_q, farther[-1]], last=(ratio_d, documents, direction, inner)
    )[0]

    loss = part
    groups = (("blk_0", "blk_3"), ("blk_2",), ("grp",), ("blk_1",))
    for axes, gate in zip(groups, (farther[n], None, farther[-1], None)):
        loss = total_over(after(loss, gate), axes)
    loss = loss[0, 0] / (rows * NZ * NX * NY * NC * lax.axis_size(GRP))
    return query_grad, doc_grad, loss


def solution(mesh):
    finer = Mesh(mesh.devices.reshape(NZ, NX, NY, NC, mesh.shape["grp"]), BLK_GRP)
    rows = P(BLK_GRP, None)
    return jax.shard_map(
        on_device,
        mesh=finer,
        in_specs=(rows, rows, rows),
        out_specs=(rows, rows, P()),
        check_vma=False,
    )
```

```python
import itertools

import jax
import jax.numpy as jnp
from jax import lax
from jax.experimental import pallas as pl
from jax.experimental.pallas import tpu as pltpu
from jax.sharding import Mesh
from jax.sharding import PartitionSpec as P

BLK = ("blk_0", "blk_1", "blk_2", "blk_3")
GRP = "grp"
BLK_GRP = BLK + (GRP,)
NZ, NX, NY, NC = 2, 4, 4, 2

SCALE = 50.0
EPSILON = 1e-06
DOC_CHUNKS = (128, 128)
QUERY_CHUNKS = (128, 128)
STRIPE = 1024
STEP = 64
MIB = 1024 * 1024


def index(z, x, y, c):
    return ((z % NZ * NX + x % NX) * NY + y % NY) * NC + c % NC


def table(target):
    pairs = []
    for at in itertools.product(range(NZ), range(NX), range(NY), range(NC)):
        to = target(*at)
        if to is not None:
            pairs.append((index(*at), index(*to)))
    return pairs


def is_edge(y, c):
    return (y == NY - 1 and c == 1) or (y == 0 and c == 0)


def off_chip(z, x, y, c):
    step = 1 if c == 1 else -1
    me = index(z, x, y, c)
    other = (me + step) % (NZ * NX * NY * NC)
    return (other // (NX * NY * NC), other // (NY * NC) % NX, other // NC % NY, other % NC)


def to_holder(z, x, y, c):
    if not is_edge(y, c):
        return None
    if c == 1:
        return (z + (x == NX - 1), x, 0, 0)
    return (z + (x == 0), x, NY - 1, 1)


def from_holder(z, x, y, c):
    if not is_edge(y, c):
        return off_chip(z, x, y, c)
    return (z, x + 1, y, c) if c == 0 else (z, x - 1, y, c)


ON_CHIP = table(lambda z, x, y, c: (z, x, y, 1 - c))
OFF_CHIP = table(off_chip)
TO_HOLDER = table(to_holder)
FROM_HOLDER = table(from_holder)
ACROSS_X = table(lambda z, x, y, c: (z, x + 2, y, c))
ACROSS_Z = table(lambda z, x, y, c: (z + 1, x, y, c))
ACROSS_XZ = table(lambda z, x, y, c: (z + 1, x + 2, y, c))


def permute(value, pairs):
    return lax.ppermute(value, BLK, pairs)


def after(value, *others):
    others = [o for o in others if o is not None]
    if not others:
        return value
    return lax.optimization_barrier((value, *others))[0]


ANY = pl.BlockSpec(memory_space=pl.ANY)
VMEM = pl.BlockSpec(memory_space=pltpu.VMEM)


def call(kernel, inputs, outputs, scratch, *, any_in, any_out):
    return pl.pallas_call(
        kernel,
        in_specs=[ANY if a else VMEM for a in any_in],
        out_specs=[ANY if a else VMEM for a in any_out],
        out_shape=outputs,
        scratch_shapes=scratch,
        cost_estimate=pl.CostEstimate(flops=1024, bytes_accessed=1024, transcendentals=0),
        compiler_params=pltpu.CompilerParams(vmem_limit_bytes=60 * MIB),
    )(*inputs)


def shape(rows, columns, kind):
    return jax.ShapeDtypeStruct((rows, columns), kind)


def start(source, target, sem):
    copy = pltpu.make_async_copy(source, target, sem)
    copy.start()
    return copy


def normalize(raw, chunks):
    rows, width = raw.shape
    spans = [(0, rows)]
    for sizes in chunks:
        spans += [(sum(sizes[:k]), size) for k, size in enumerate(sizes)]
    n, steps = len(spans), rows // STEP

    def kernel(raw, *refs):
        outs, ratio = refs[:n], refs[n]
        before, result, sems, out_sems = refs[n + 1 :]
        loads = [
            start(raw.at[pl.ds(k * STEP, STEP)], before.at[pl.ds(k * STEP, STEP)], sems.at[k])
            for k in range(steps)
        ]
        stores = []
        for k in range(steps):
            own = pl.ds(k * STEP, STEP)
            loads[k].wait()
            wide = before[own].astype(jnp.float32)
            scale = lax.rsqrt(jnp.sum(wide * wide, axis=-1, keepdims=True) + EPSILON)
            ratio[own] = scale
            result[own] = (wide * scale).astype(jnp.bfloat16)
            for j, (at, size) in enumerate(spans):
                if k * STEP < at + size <= (k + 1) * STEP:
                    stores.append(start(result.at[pl.ds(at, size)], outs[j], out_sems.at[j]))
        for copy in stores:
            copy.wait()

    kind = jnp.bfloat16
    return call(
        kernel,
        [raw],
        [shape(size, width, kind) for _, size in spans] + [shape(rows, 1, jnp.float32)],
        [
            pltpu.VMEM((rows, width), kind),
            pltpu.VMEM((rows, width), kind),
            pltpu.SemaphoreType.DMA((steps,)),
            pltpu.SemaphoreType.DMA((n,)),
        ],
        any_in=[True],
        any_out=[True] * n + [False],
    )


def places(blocks):
    at, found = 0, []
    for block in blocks:
        found.append((at, block.shape[0]))
        at += block.shape[0]
    return found, at


def diagonal(size):
    return lax.broadcasted_iota(jnp.int32, (size, size), 0) == lax.broadcasted_iota(
        jnp.int32, (size, size), 1
    )


def column_of(row):
    return jnp.sum(jnp.where(diagonal(row.shape[1]), row, 0), axis=1, keepdims=True)


def row_of(column):
    return jnp.sum(jnp.where(diagonal(column.shape[0]), column, 0), axis=0, keepdims=True)


def scores_of(own, block):
    return SCALE * lax.dot_general(
        own, block, (((1,), (1,)), ((), ())), preferred_element_type=jnp.float32
    )


def groups_of(found, rows):
    runs = []
    for k, (at, size) in enumerate(found):
        if runs and at + size - runs[-1][1] <= rows:
            runs[-1] = (runs[-1][0] + [k], runs[-1][1], at + size - runs[-1][1])
        else:
            runs.append(([k], at, size))
    return runs


def query_side(norm, positive, blocks):
    rows, width = norm.shape
    found, depth = places(blocks)
    n = len(blocks)

    def kernel(norm, positive, *refs):
        blocks, (lse_out, part_out, weights_out, inner_out) = refs[:n], refs[n : n + 4]
        own, buffer, scores, sems = refs[n + 4 :]
        first = start(norm, own, sems.at[n])
        loads = [
            start(blocks[k], buffer.at[pl.ds(at, size)], sems.at[k])
            for k, (at, size) in enumerate(found)
        ]
        first.wait()
        total = jnp.zeros((rows, 1), jnp.float32)
        for members, at, size in groups_of(found, rows):
            for k in members:
                loads[k].wait()
            here = scores_of(own[...], buffer[at : at + size])
            scores[:, at : at + size] = here
            total += jnp.sum(jnp.exp(here), axis=-1, keepdims=True)
        lse = jnp.log(total)
        lse_out[...] = row_of(lse)
        target = column_of(positive[...])
        spos = jnp.zeros((rows, 1), jnp.float32)
        inner = jnp.zeros((rows, 1), jnp.float32)
        for at in range(0, depth, rows):
            here = scores[:, at : at + rows]
            weights = jnp.exp(here - lse)
            if at < 2 * rows:
                hot = lax.broadcasted_iota(jnp.int32, (rows, rows), 1) + at == target
                hot = hot.astype(jnp.float32)
                spos += jnp.sum(here * hot, axis=-1, keepdims=True)
                weights = weights - hot
            weights = weights.astype(jnp.bfloat16)
            weights_out[:, at : at + rows] = weights
            inner += jnp.sum(weights.astype(jnp.float32) * here, axis=-1, keepdims=True)
        inner_out[...] = inner
        part = jnp.sum(lse - spos, axis=0, keepdims=True)
        part_out[...] = jnp.broadcast_to(part, part_out.shape)

    return call(
        kernel,
        [norm, positive, *blocks],
        [
            shape(1, rows, jnp.float32),
            shape(8, 128, jnp.float32),
            shape(rows, depth, jnp.bfloat16),
            shape(rows, 1, jnp.float32),
        ],
        [
            pltpu.VMEM((rows, width), jnp.bfloat16),
            pltpu.VMEM((depth, width), jnp.bfloat16),
            pltpu.VMEM((rows, depth), jnp.float32),
            pltpu.SemaphoreType.DMA((n + 1,)),
        ],
        any_in=[True, False] + [True] * n,
        any_out=[False] * 4,
    )


def query_gradient(weights, inner, ratio, raw, blocks):
    rows, width = raw.shape
    found, depth = places(blocks)
    n, stripes = len(blocks), width // STRIPE

    def kernel(weights, inner, ratio, raw, *refs):
        blocks, out, done = refs[:n], refs[n], refs[n + 1]
        buffer, wide, result, sems, out_sems = refs[n + 2 :]
        done[...] = jnp.zeros_like(done)
        loads = []
        for s in range(stripes):
            at_s = pl.ds(s * STRIPE, STRIPE)
            loads.append(
                [
                    start(blocks[k].at[:, at_s], buffer.at[pl.ds(at, size), at_s], sems.at[s, k])
                    for k, (at, size) in enumerate(found)
                ]
                + [start(raw.at[:, at_s], wide.at[:, at_s], sems.at[s, n])]
            )
        gain = SCALE * ratio[...]
        coef = ratio[...] * ratio[...] * inner[...]
        stores = []
        for s in range(stripes):
            here = slice(s * STRIPE, (s + 1) * STRIPE)
            for copy in loads[s]:
                copy.wait()
            direction = jnp.dot(weights[...], buffer[:, here], preferred_element_type=jnp.float32)
            result[:, here] = gain * direction - coef * wide[:, here].astype(jnp.float32)
            at_s = pl.ds(s * STRIPE, STRIPE)
            stores.append(start(result.at[:, at_s], out.at[:, at_s], out_sems.at[s]))
        for copy in stores:
            copy.wait()

    return call(
        kernel,
        [weights, inner, ratio, raw, *blocks],
        [shape(rows, width, jnp.float32), shape(8, 128, jnp.float32)],
        [
            pltpu.VMEM((depth, width), jnp.bfloat16),
            pltpu.VMEM((rows, width), jnp.bfloat16),
            pltpu.VMEM((rows, width), jnp.float32),
            pltpu.SemaphoreType.DMA((stripes, n + 1)),
            pltpu.SemaphoreType.DMA((stripes,)),
        ],
        any_in=[False] * 3 + [True] * (n + 1),
        any_out=[True, False],
    )


def document_side(norm, positive, lses, blocks, last=None):
    rows, width = norm.shape
    found, depth = places(blocks)
    n, stripes = len(blocks), width // STRIPE
    given = [] if positive is None else [positive]
    small = given + [lses] + ([] if last is None else [last[0], last[3]])
    large = [norm, *blocks] + ([] if last is None else [last[1], last[2]])
    m = len(small)

    def kernel(*refs):
        smalls, (norm, *blocks) = refs[:m], refs[m : m + 1 + n]
        rest = refs[m + 1 + n :]
        lses = smalls[len(given)]
        if last is not None:
            ratio, before_inner = smalls[-2:]
            raw, before = rest[:2]
            rest = rest[2:]
        out, rest = rest[0], rest[1:]
        if last is None:
            inner_out, rest = rest[0], rest[1:]
        own, buffer, result, wide, sems, more_sems, out_sems = rest
        first = start(norm, own, sems.at[n])
        loads = [
            start(blocks[k], buffer.at[pl.ds(at, size)], sems.at[k])
            for k, (at, size) in enumerate(found)
        ]
        more = []
        if last is not None:
            for s in range(stripes):
                at_s = pl.ds(s * STRIPE, STRIPE)
                more.append(
                    [
                        start(raw.at[:, at_s], wide.at[:, at_s], more_sems.at[s, 0]),
                        start(before.at[:, at_s], result.at[:, at_s], more_sems.at[s, 1]),
                    ]
                )
        first.wait()
        inner = jnp.zeros((rows, 1), jnp.float32) if last is None else before_inner[...]
        weights = []
        for members, at, size in groups_of(found, rows):
            for k in members:
                loads[k].wait()
            here = scores_of(own[...], buffer[at : at + size])
            weight = jnp.exp(here - lses[:, at : at + size])
            if at < 2 * rows and given:
                hot = lax.broadcasted_iota(jnp.int32, (rows, size), 0)
                hot = hot == smalls[0][:, at : at + size]
                weight = weight - hot.astype(jnp.float32)
            weight = weight.astype(jnp.bfloat16)
            inner += jnp.sum(weight.astype(jnp.float32) * here, axis=-1, keepdims=True)
            weights.append((weight, at, size))
        if last is None:
            inner_out[...] = inner
        else:
            gain = SCALE * ratio[...]
            coef = ratio[...] * ratio[...] * inner
        stores = []
        for s in range(stripes):
            here = slice(s * STRIPE, (s + 1) * STRIPE)
            direction = None
            for weight, at, size in weights:
                term = jnp.dot(
                    weight, buffer[at : at + size, here], preferred_element_type=jnp.float32
                )
                direction = term if direction is None else direction + term
            if last is not None:
                for copy in more[s]:
                    copy.wait()
                direction = gain * (direction + result[:, here])
                direction = direction - coef * wide[:, here].astype(jnp.float32)
            result[:, here] = direction
            at_s = pl.ds(s * STRIPE, STRIPE)
            stores.append(start(result.at[:, at_s], out.at[:, at_s], out_sems.at[s]))
        for copy in stores:
            copy.wait()

    outputs = [shape(rows, width, jnp.float32)]
    if last is None:
        outputs.append(shape(rows, 1, jnp.float32))
    return call(
        kernel,
        small + large,
        outputs,
        [
            pltpu.VMEM((rows, width), jnp.bfloat16),
            pltpu.VMEM((depth, width), jnp.bfloat16),
            pltpu.VMEM((rows, width), jnp.float32),
            pltpu.VMEM((rows, width), jnp.bfloat16),
            pltpu.SemaphoreType.DMA((n + 1,)),
            pltpu.SemaphoreType.DMA((stripes, 2)),
            pltpu.SemaphoreType.DMA((stripes,)),
        ],
        any_in=[False] * m + [True] * len(large),
        any_out=[True] + [False] * (last is None),
    )


def total_over(value, axes):
    count = 1
    for axis in axes:
        count *= lax.axis_size(axis)
    parts = [
        lax.ppermute(value, axes, [(s, (s + step) % count) for s in range(count)])
        for step in range(1, count)
    ]
    for part in parts:
        value = value + part
    return value


def on_device(queries, documents, positives):
    rows = queries.shape[0]
    y = lax.axis_index("blk_2")
    c = lax.axis_index("blk_3")
    edge = ((y == NY - 1) & (c == 1)) | ((y == 0) & (c == 0))
    n, tail = len(DOC_CHUNKS), QUERY_CHUNKS[-1]
    halves = (rows // 2, rows // 2)

    norm_d, *pieces_d, ratio_d = normalize(documents, [DOC_CHUNKS, halves])
    norm_q, *pieces_q, ratio_q = normalize(queries, [QUERY_CHUNKS])
    halves_d, pieces_d = pieces_d[-2:], pieces_d[:-2]

    core_d = permute(norm_d, ON_CHIP)
    core_q = permute(norm_q, ON_CHIP)

    far, farther = [], []
    for k, part in enumerate(pieces_d + pieces_q):
        gates = [] if k < 2 else far[:2] + farther[:1]
        far.append(permute(after(part, *gates), ACROSS_X))
        farther.append(permute(far[k], ACROSS_Z))

    held_d = permute(halves_d[1], TO_HOLDER)
    near_d = [
        permute(after(halves_d[0], far[1]), OFF_CHIP),
        permute(after(jnp.where(edge, held_d, halves_d[1]), far[1]), FROM_HOLDER),
    ]
    held_q = permute(after(norm_q, held_d, core_d, core_q), TO_HOLDER)
    near_q = permute(after(jnp.where(edge, held_q, norm_q), far[-1]), FROM_HOLDER)

    docs = [norm_d, core_d, *near_d] + far[:n] + farther[:n]
    lse, part, weights, inner = query_side(norm_q, positives, docs)

    message = after(lse, farther[n])
    other = permute(message, ON_CHIP)
    near_lse = permute(message, OFF_CHIP)
    far_lse = permute(message, ACROSS_X)
    farther_lse = permute(message, ACROSS_XZ)
    marks = jnp.concatenate([positives, jnp.full_like(positives, -1)], axis=1)

    query_grad, done = query_gradient(weights, inner, ratio_q, queries, docs)
    early = jnp.concatenate([lse, other, far_lse, farther_lse[:, :-tail]], axis=1)
    early = after(early, query_grad)
    direction, inner = document_side(norm_d, marks, early, [norm_q, core_q] + far[n:] + farther[n:-1])
    late = jnp.concatenate([near_lse, farther_lse[:, -tail:]], axis=1)
    doc_grad = document_side(
        norm_d, None, late, [near_q, farther[-1]], last=(ratio_d, documents, direction, inner)
    )[0]

    loss = part
    groups = (("blk_0", "blk_3"), ("blk_2",), ("grp",), ("blk_1",))
    for axes, gate in zip(groups, (farther[n], None, farther[-1], None)):
        loss = total_over(after(loss, gate), axes)
    loss = loss[0, 0] / (rows * NZ * NX * NY * NC * lax.axis_size(GRP))
    return query_grad, doc_grad, loss


def solution(mesh):
    finer = Mesh(mesh.devices.reshape(NZ, NX, NY, NC, mesh.shape["grp"]), BLK_GRP)
    rows = P(BLK_GRP, None)
    return jax.shard_map(
        on_device,
        mesh=finer,
        in_specs=(rows, rows, rows),
        out_specs=(rows, rows, P()),
        check_vma=False,
    )
```

```python
import itertools

import jax
import jax.numpy as jnp
from jax import lax
from jax.experimental import pallas as pl
from jax.experimental.pallas import tpu as pltpu
from jax.sharding import Mesh
from jax.sharding import PartitionSpec as P

BLK = ("blk_0", "blk_1", "blk_2", "blk_3")
GRP = "grp"
BLK_GRP = BLK + (GRP,)
NZ, NX, NY, NC = 2, 4, 4, 2

SCALE = 50.0
EPSILON = 1e-06
DOC_CHUNKS = (128, 128)
QUERY_CHUNKS = (128, 128)
STRIPE = 1024
STEP = 64
MIB = 1024 * 1024


def index(z, x, y, c):
    return ((z % NZ * NX + x % NX) * NY + y % NY) * NC + c % NC


def table(target):
    pairs = []
    for at in itertools.product(range(NZ), range(NX), range(NY), range(NC)):
        to = target(*at)
        if to is not None:
            pairs.append((index(*at), index(*to)))
    return pairs


def is_edge(y, c):
    return (y == NY - 1 and c == 1) or (y == 0 and c == 0)


def off_chip(z, x, y, c):
    step = 1 if c == 1 else -1
    me = index(z, x, y, c)
    other = (me + step) % (NZ * NX * NY * NC)
    return (other // (NX * NY * NC), other // (NY * NC) % NX, other // NC % NY, other % NC)


def to_holder(z, x, y, c):
    if not is_edge(y, c):
        return None
    if c == 1:
        return (z + (x == NX - 1), x, 0, 0)
    return (z + (x == 0), x, NY - 1, 1)


def from_holder(z, x, y, c):
    if not is_edge(y, c):
        return off_chip(z, x, y, c)
    return (z, x + 1, y, c) if c == 0 else (z, x - 1, y, c)


ON_CHIP = table(lambda z, x, y, c: (z, x, y, 1 - c))
OFF_CHIP = table(off_chip)
TO_HOLDER = table(to_holder)
FROM_HOLDER = table(from_holder)
ACROSS_X = table(lambda z, x, y, c: (z, x + 2, y, c))
ACROSS_Z = table(lambda z, x, y, c: (z + 1, x, y, c))
ACROSS_XZ = table(lambda z, x, y, c: (z + 1, x + 2, y, c))


def permute(value, pairs):
    return lax.ppermute(value, BLK, pairs)


def after(value, *others):
    others = [o for o in others if o is not None]
    if not others:
        return value
    return lax.optimization_barrier((value, *others))[0]


ANY = pl.BlockSpec(memory_space=pl.ANY)
VMEM = pl.BlockSpec(memory_space=pltpu.VMEM)


def call(kernel, inputs, outputs, scratch, *, any_in, any_out):
    return pl.pallas_call(
        kernel,
        in_specs=[ANY if a else VMEM for a in any_in],
        out_specs=[ANY if a else VMEM for a in any_out],
        out_shape=outputs,
        scratch_shapes=scratch,
        cost_estimate=pl.CostEstimate(flops=1024, bytes_accessed=1024, transcendentals=0),
        compiler_params=pltpu.CompilerParams(vmem_limit_bytes=60 * MIB),
    )(*inputs)


def shape(rows, columns, kind):
    return jax.ShapeDtypeStruct((rows, columns), kind)


def start(source, target, sem):
    copy = pltpu.make_async_copy(source, target, sem)
    copy.start()
    return copy


def normalize(raw, chunks):
    rows, width = raw.shape
    spans = [(0, rows)]
    for sizes in chunks:
        spans += [(sum(sizes[:k]), size) for k, size in enumerate(sizes)]
    n, steps = len(spans), rows // STEP

    def kernel(raw, *refs):
        outs, ratio = refs[:n], refs[n]
        before, result, sems, out_sems = refs[n + 1 :]
        loads = [
            start(raw.at[pl.ds(k * STEP, STEP)], before.at[pl.ds(k * STEP, STEP)], sems.at[k])
            for k in range(steps)
        ]
        stores = []
        for k in range(steps):
            own = pl.ds(k * STEP, STEP)
            loads[k].wait()
            wide = before[own].astype(jnp.float32)
            scale = lax.rsqrt(jnp.sum(wide * wide, axis=-1, keepdims=True) + EPSILON)
            ratio[own] = scale
            result[own] = (wide * scale).astype(jnp.bfloat16)
            for j, (at, size) in enumerate(spans):
                if k * STEP < at + size <= (k + 1) * STEP:
                    stores.append(start(result.at[pl.ds(at, size)], outs[j], out_sems.at[j]))
        for copy in stores:
            copy.wait()

    kind = jnp.bfloat16
    return call(
        kernel,
        [raw],
        [shape(size, width, kind) for _, size in spans] + [shape(rows, 1, jnp.float32)],
        [
            pltpu.VMEM((rows, width), kind),
            pltpu.VMEM((rows, width), kind),
            pltpu.SemaphoreType.DMA((steps,)),
            pltpu.SemaphoreType.DMA((n,)),
        ],
        any_in=[True],
        any_out=[True] * n + [False],
    )


def places(blocks):
    at, found = 0, []
    for block in blocks:
        found.append((at, block.shape[0]))
        at += block.shape[0]
    return found, at


def diagonal(size):
    return lax.broadcasted_iota(jnp.int32, (size, size), 0) == lax.broadcasted_iota(
        jnp.int32, (size, size), 1
    )


def column_of(row):
    return jnp.sum(jnp.where(diagonal(row.shape[1]), row, 0), axis=1, keepdims=True)


def row_of(column):
    return jnp.sum(jnp.where(diagonal(column.shape[0]), column, 0), axis=0, keepdims=True)


def scores_of(own, block):
    return SCALE * lax.dot_general(
        own, block, (((1,), (1,)), ((), ())), preferred_element_type=jnp.float32
    )


def groups_of(found, rows):
    runs = []
    for k, (at, size) in enumerate(found):
        if runs and at + size - runs[-1][1] <= rows:
            runs[-1] = (runs[-1][0] + [k], runs[-1][1], at + size - runs[-1][1])
        else:
            runs.append(([k], at, size))
    return runs


def query_side(norm, positive, blocks):
    rows, width = norm.shape
    found, depth = places(blocks)
    n = len(blocks)

    def kernel(norm, positive, *refs):
        blocks, (lse_out, part_out, weights_out, inner_out) = refs[:n], refs[n : n + 4]
        own, buffer, scores, sems = refs[n + 4 :]
        first = start(norm, own, sems.at[n])
        loads = [
            start(blocks[k], buffer.at[pl.ds(at, size)], sems.at[k])
            for k, (at, size) in enumerate(found)
        ]
        first.wait()
        total = jnp.zeros((rows, 1), jnp.float32)
        for members, at, size in groups_of(found, rows):
            for k in members:
                loads[k].wait()
            here = scores_of(own[...], buffer[at : at + size])
            scores[:, at : at + size] = here
            total += jnp.sum(jnp.exp(here), axis=-1, keepdims=True)
        lse = jnp.log(total)
        lse_out[...] = row_of(lse)
        target = column_of(positive[...])
        spos = jnp.zeros((rows, 1), jnp.float32)
        inner = jnp.zeros((rows, 1), jnp.float32)
        for at in range(0, depth, rows):
            here = scores[:, at : at + rows]
            weights = jnp.exp(here - lse)
            if at < 2 * rows:
                hot = lax.broadcasted_iota(jnp.int32, (rows, rows), 1) + at == target
                hot = hot.astype(jnp.float32)
                spos += jnp.sum(here * hot, axis=-1, keepdims=True)
                weights = weights - hot
            weights = weights.astype(jnp.bfloat16)
            weights_out[:, at : at + rows] = weights
            inner += jnp.sum(weights.astype(jnp.float32) * here, axis=-1, keepdims=True)
        inner_out[...] = inner
        part = jnp.sum(lse - spos, axis=0, keepdims=True)
        part_out[...] = jnp.broadcast_to(part, part_out.shape)

    return call(
        kernel,
        [norm, positive, *blocks],
        [
            shape(1, rows, jnp.float32),
            shape(8, 128, jnp.float32),
            shape(rows, depth, jnp.bfloat16),
            shape(rows, 1, jnp.float32),
        ],
        [
            pltpu.VMEM((rows, width), jnp.bfloat16),
            pltpu.VMEM((depth, width), jnp.bfloat16),
            pltpu.VMEM((rows, depth), jnp.float32),
            pltpu.SemaphoreType.DMA((n + 1,)),
        ],
        any_in=[True, False] + [True] * n,
        any_out=[False] * 4,
    )


def query_gradient(weights, inner, ratio, raw, blocks):
    rows, width = raw.shape
    found, depth = places(blocks)
    n, stripes = len(blocks), width // STRIPE

    def kernel(weights, inner, ratio, raw, *refs):
        blocks, out, done = refs[:n], refs[n], refs[n + 1]
        buffer, wide, result, sems, out_sems = refs[n + 2 :]
        done[...] = jnp.zeros_like(done)
        loads = []
        for s in range(stripes):
            at_s = pl.ds(s * STRIPE, STRIPE)
            loads.append(
                [
                    start(blocks[k].at[:, at_s], buffer.at[pl.ds(at, size), at_s], sems.at[s, k])
                    for k, (at, size) in enumerate(found)
                ]
                + [start(raw.at[:, at_s], wide.at[:, at_s], sems.at[s, n])]
            )
        gain = SCALE * ratio[...]
        coef = ratio[...] * ratio[...] * inner[...]
        stores = []
        for s in range(stripes):
            here = slice(s * STRIPE, (s + 1) * STRIPE)
            for copy in loads[s]:
                copy.wait()
            direction = jnp.dot(weights[...], buffer[:, here], preferred_element_type=jnp.float32)
            result[:, here] = gain * direction - coef * wide[:, here].astype(jnp.float32)
            at_s = pl.ds(s * STRIPE, STRIPE)
            stores.append(start(result.at[:, at_s], out.at[:, at_s], out_sems.at[s]))
        for copy in stores:
            copy.wait()

    return call(
        kernel,
        [weights, inner, ratio, raw, *blocks],
        [shape(rows, width, jnp.float32), shape(8, 128, jnp.float32)],
        [
            pltpu.VMEM((depth, width), jnp.bfloat16),
            pltpu.VMEM((rows, width), jnp.bfloat16),
            pltpu.VMEM((rows, width), jnp.float32),
            pltpu.SemaphoreType.DMA((stripes, n + 1)),
            pltpu.SemaphoreType.DMA((stripes,)),
        ],
        any_in=[False] * 3 + [True] * (n + 1),
        any_out=[True, False],
    )


def document_side(norm, positive, lses, blocks, last=None):
    rows, width = norm.shape
    found, depth = places(blocks)
    n, stripes = len(blocks), width // STRIPE
    given = [] if positive is None else [positive]
    small = given + [lses] + ([] if last is None else [last[0], last[3]])
    large = [norm, *blocks] + ([] if last is None else [last[1], last[2]])
    m = len(small)

    def kernel(*refs):
        smalls, (norm, *blocks) = refs[:m], refs[m : m + 1 + n]
        rest = refs[m + 1 + n :]
        lses = smalls[len(given)]
        if last is not None:
            ratio, before_inner = smalls[-2:]
            raw, before = rest[:2]
            rest = rest[2:]
        out, rest = rest[0], rest[1:]
        if last is None:
            inner_out, rest = rest[0], rest[1:]
        own, buffer, result, wide, sems, more_sems, out_sems = rest
        first = start(norm, own, sems.at[n])
        loads = [
            start(blocks[k], buffer.at[pl.ds(at, size)], sems.at[k])
            for k, (at, size) in enumerate(found)
        ]
        more = []
        if last is not None:
            for s in range(stripes):
                at_s = pl.ds(s * STRIPE, STRIPE)
                more.append(
                    [
                        start(raw.at[:, at_s], wide.at[:, at_s], more_sems.at[s, 0]),
                        start(before.at[:, at_s], result.at[:, at_s], more_sems.at[s, 1]),
                    ]
                )
        first.wait()
        inner = jnp.zeros((rows, 1), jnp.float32) if last is None else before_inner[...]
        weights = []
        for members, at, size in groups_of(found, rows):
            for k in members:
                loads[k].wait()
            here = scores_of(own[...], buffer[at : at + size])
            weight = jnp.exp(here - lses[:, at : at + size])
            if at < 2 * rows and given:
                hot = lax.broadcasted_iota(jnp.int32, (rows, size), 0)
                hot = hot == smalls[0][:, at : at + size]
                weight = weight - hot.astype(jnp.float32)
            weight = weight.astype(jnp.bfloat16)
            inner += jnp.sum(weight.astype(jnp.float32) * here, axis=-1, keepdims=True)
            weights.append((weight, at, size))
        if last is None:
            inner_out[...] = inner
        else:
            gain = SCALE * ratio[...]
            coef = ratio[...] * ratio[...] * inner
        stores = []
        for s in range(stripes):
            here = slice(s * STRIPE, (s + 1) * STRIPE)
            direction = None
            for weight, at, size in weights:
                term = jnp.dot(
                    weight, buffer[at : at + size, here], preferred_element_type=jnp.float32
                )
                direction = term if direction is None else direction + term
            if last is not None:
                for copy in more[s]:
                    copy.wait()
                direction = gain * (direction + result[:, here])
                direction = direction - coef * wide[:, here].astype(jnp.float32)
            result[:, here] = direction
            at_s = pl.ds(s * STRIPE, STRIPE)
            stores.append(start(result.at[:, at_s], out.at[:, at_s], out_sems.at[s]))
        for copy in stores:
            copy.wait()

    outputs = [shape(rows, width, jnp.float32)]
    if last is None:
        outputs.append(shape(rows, 1, jnp.float32))
    return call(
        kernel,
        small + large,
        outputs,
        [
            pltpu.VMEM((rows, width), jnp.bfloat16),
            pltpu.VMEM((depth, width), jnp.bfloat16),
            pltpu.VMEM((rows, width), jnp.float32),
            pltpu.VMEM((rows, width), jnp.bfloat16),
            pltpu.SemaphoreType.DMA((n + 1,)),
            pltpu.SemaphoreType.DMA((stripes, 2)),
            pltpu.SemaphoreType.DMA((stripes,)),
        ],
        any_in=[False] * m + [True] * len(large),
        any_out=[True] + [False] * (last is None),
    )


def total_over(value, axes):
    count = 1
    for axis in axes:
        count *= lax.axis_size(axis)
    parts = [
        lax.ppermute(value, axes, [(s, (s + step) % count) for s in range(count)])
        for step in range(1, count)
    ]
    for part in parts:
        value = value + part
    return value


def on_device(queries, documents, positives):
    rows = queries.shape[0]
    y = lax.axis_index("blk_2")
    c = lax.axis_index("blk_3")
    edge = ((y == NY - 1) & (c == 1)) | ((y == 0) & (c == 0))
    n, tail = len(DOC_CHUNKS), QUERY_CHUNKS[-1]
    halves = (rows // 2, rows // 2)

    norm_d, *pieces_d, ratio_d = normalize(documents, [DOC_CHUNKS, halves])
    norm_q, *pieces_q, ratio_q = normalize(queries, [QUERY_CHUNKS])
    halves_d, pieces_d = pieces_d[-2:], pieces_d[:-2]

    core_d = permute(norm_d, ON_CHIP)
    core_q = permute(norm_q, ON_CHIP)

    far, farther = [], []
    for k, part in enumerate(pieces_d + pieces_q):
        gates = [] if k < 2 else far[:2] + farther[:1]
        far.append(permute(after(part, *gates), ACROSS_X))
        farther.append(permute(far[k], ACROSS_Z))

    held_d = permute(halves_d[1], TO_HOLDER)
    near_d = [
        permute(after(halves_d[0], far[1]), OFF_CHIP),
        permute(after(jnp.where(edge, held_d, halves_d[1]), far[1]), FROM_HOLDER),
    ]
    held_q = permute(after(norm_q, held_d, core_d, core_q), TO_HOLDER)

    docs = [norm_d, core_d, *near_d] + far[:n] + farther[:n]
    lse, part, weights, inner = query_side(after(norm_q, far[-1]), positives, docs)

    near_q = permute(after(jnp.where(edge, held_q, norm_q), far[-1], lse), FROM_HOLDER)
    message = after(lse, farther[n])
    other = permute(message, ON_CHIP)
    near_lse = permute(message, OFF_CHIP)
    far_lse = permute(message, ACROSS_X)
    farther_lse = permute(message, ACROSS_XZ)
    marks = jnp.concatenate([positives, jnp.full_like(positives, -1)], axis=1)

    query_grad, done = query_gradient(weights, inner, ratio_q, queries, docs)
    early = jnp.concatenate([lse, other, far_lse, farther_lse[:, :-tail]], axis=1)
    early = after(early, query_grad)
    direction, inner = document_side(norm_d, marks, early, [norm_q, core_q] + far[n:] + farther[n:-1])
    late = jnp.concatenate([near_lse, farther_lse[:, -tail:]], axis=1)
    doc_grad = document_side(
        norm_d, None, late, [near_q, farther[-1]], last=(ratio_d, documents, direction, inner)
    )[0]

    loss = part
    groups = (("blk_0", "blk_3"), ("blk_2",), ("grp",), ("blk_1",))
    for axes, gate in zip(groups, (far_lse, None, inner, None)):
        loss = total_over(after(loss, gate), axes)
    loss = loss[0, 0] / (rows * NZ * NX * NY * NC * lax.axis_size(GRP))
    return query_grad, doc_grad, loss


def solution(mesh):
    finer = Mesh(mesh.devices.reshape(NZ, NX, NY, NC, mesh.shape["grp"]), BLK_GRP)
    rows = P(BLK_GRP, None)
    return jax.shard_map(
        on_device,
        mesh=finer,
        in_specs=(rows, rows, rows),
        out_specs=(rows, rows, P()),
        check_vma=False,
    )
```
